512 devices in a mesh: snap: 16 (over z), vert: 32 (over y, x, core).
Axes of the slice: x: 4, y: 4, z: 16, core: 2. Of those that a mesh axis runs over, the one named last changes fastest.
Arguments:
- features: bfloat16 [16, 24576, 128], P('snap', 'vert'), may hold values from -6 to 6
- adjacency_tiles: bfloat16 [16, 384, 128, 128], P('snap', 'vert'), may hold values from -0.375 to 0.375
- src_block: int32 [16, 384], P('snap', 'vert'), may hold values from 0 to 191, as said below
- dst_block: int32 [16, 384], P('snap', 'vert'), may hold values from 0 to 5
- block_count: int32 [16, 32], P('snap', 'vert'), may hold values from 6 to 12, as said below
- w_conv: bfloat16 [128, 512], replicated, may hold values from -0.5 to 0.5
- b_conv: float32 [512], replicated, may hold values from -3 to 3
- w_input: bfloat16 [512, 2048], replicated, may hold values from -0.25 to 0.25
- w_state: bfloat16 [512, 2048], replicated, may hold values from -0.25 to 0.25
- b_gates: float32 [2048], replicated, may hold values from -3 to 3
Outputs:
- hidden_seq: bfloat16 [16, 24576, 512], P('snap', 'vert')
The draws below stay inside these ranges and needn't reach their ends.
Inputs may be any that keep to these rules, and one draw needn't show every extreme that they name: `src_block`: slot s of owner v names a column block held by owner v - 1, v or v + 1 (clipped to the owners that exist); its first slot names one of owner v - 1 and its second one of owner v + 1 where those exist. `block_count`: in every snapshot some owner has all 12 slots live.
All inputs are finite; a program needn't handle non-finite values.
Results may differ from the reference program's by a relative error of at most 0.0044.
Values may be sent and summed in bfloat16 or wider, within the bound.
A program may use at most 64 MiB of HBM per device.

```python
import jax
import jax.numpy as jnp
from jax import lax

F = 128
P_SIZE = 512
HID = 512
BLOCK = 128
V_DEV = 768
SNAPS = 16
VERTS = 24576
RBLK = 6
EBLK = 12
N_VERT = 32


def draw_src_block(key, part):
    owners = VERTS // V_DEV
    shape = (SNAPS, owners, EBLK)
    owner_grid = jnp.broadcast_to(jnp.arange(owners, dtype=jnp.int32)[None, :, None], shape)
    offsets = jax.random.randint(jax.random.fold_in(key, 11), shape, -1, 2)
    slot_grid = jnp.broadcast_to(jnp.arange(EBLK, dtype=jnp.int32)[None, None, :], shape)
    offsets = jnp.where(slot_grid == 0, -1, jnp.where(slot_grid == 1, 1, offsets))
    target = jnp.clip(owner_grid + offsets, 0, owners - 1)
    within = jax.random.randint(jax.random.fold_in(key, 12), shape, 0, RBLK)
    return (target * RBLK + within).reshape(SNAPS, owners * EBLK).astype(jnp.int32)


def draw_block_count(key, part):
    owners = VERTS // V_DEV
    lowest = max(2, EBLK // 2)
    counts = jax.random.randint(jax.random.fold_in(key, 21), (SNAPS, owners), lowest, EBLK + 1)
    fullest = jax.random.randint(jax.random.fold_in(key, 22), (SNAPS, 1), 0, owners)
    columns = jnp.arange(owners, dtype=jnp.int32)[None, :]
    return jnp.where(columns == fullest, EBLK, counts).astype(jnp.int32)


def set_ends(drawn, stream_key, least, top_value):
    dims = drawn.shape
    place = [jax.random.randint(jax.random.fold_in(stream_key, axis), (), 0, dims[axis]) for axis in range(len(dims))]
    drawn = drawn.at[tuple(place)].set(least)
    longest = dims.index(max(dims))
    place[longest] = (place[longest] + 1) % dims[longest]
    return drawn.at[tuple(place)].set(top_value)


def steps_of(stream_key, shape, split, low, top_value):
    loudness, own = 1.0, jax.random.fold_in(stream_key, 6)
    for dim, shards_of in split:
        draws = jnp.exp(jax.random.uniform(jax.random.fold_in(own, dim), (shards_of,), jnp.float32, low / len(split), top_value / len(split)))
        loudness = loudness * jnp.repeat(draws, shape[dim] // shards_of).reshape([-1 if axis == dim else 1 for axis in range(len(shape))])
    return loudness


def centred(own_key, extent, spread, most, cuts=(), kind=jnp.bfloat16):
    drawn = jax.random.normal(own_key, extent, jnp.float32) * spread
    if len(cuts) > 0:
        drawn = steps_of(own_key, extent, cuts, -0.22, 0.18) * drawn
    return jnp.clip(drawn, min=-most, max=most).astype(kind)


def setup_inputs(seed: int = 0) -> dict:
    seeds = jax.random.split(jax.random.key(seed), 11)
    features = centred(seeds[0], (SNAPS, VERTS, F), 1.0, 6.0, ((0, 16), (1, 32)))
    adjacency_tiles = centred(seeds[1], (SNAPS, N_VERT * EBLK, BLOCK, BLOCK), (2 * BLOCK) ** -0.5, 0.375, ((0, 16), (1, 32)))
    src_block = draw_src_block(jax.random.fold_in(seeds[10], 71), 0)
    dst_block = set_ends(jax.random.randint(seeds[3], (SNAPS, N_VERT * EBLK), 0, RBLK), jax.random.fold_in(seeds[3], 1), 0, RBLK - 1).astype(jnp.int32)
    block_count = draw_block_count(jax.random.fold_in(seeds[10], 71), 0)
    w_conv = centred(seeds[5], (F, P_SIZE), F ** -0.5, 0.5)
    b_conv = centred(seeds[6], (P_SIZE,), 0.5, 3.0, (), jnp.float32)
    w_input = centred(seeds[7], (P_SIZE, 4 * HID), P_SIZE ** -0.5, 0.25)
    w_state = centred(seeds[8], (HID, 4 * HID), HID ** -0.5, 0.25)
    b_gates = centred(seeds[9], (4 * HID,), 0.5, 3.0, (), jnp.float32)
    return {"features": features, "adjacency_tiles": adjacency_tiles, "src_block": src_block, "dst_block": dst_block, "block_count": block_count, "w_conv": w_conv, "b_conv": b_conv, "w_input": w_input, "w_state": w_state, "b_gates": b_gates}


forget_bias = 2.0


def reference(features, adjacency_tiles, src_block, dst_block, block_count, w_conv, b_conv, w_input, w_state, b_gates):
    owners = VERTS // V_DEV
    nblocks = VERTS // BLOCK
    slots = jnp.arange(owners * EBLK, dtype=jnp.int32)
    owner_of = slots // EBLK
    position = slots % EBLK

    def advance(carry, inputs):
        hidden, cell = carry
        feats, tiles_now, sources, targets, counts = inputs
        blocks = feats.reshape(nblocks, BLOCK, F)
        picked = blocks[sources]
        product = jnp.einsum('ebk,ekf->ebf', tiles_now.astype(jnp.float32), picked.astype(jnp.float32), precision=lax.Precision.HIGHEST)
        alive = (position < counts[owner_of]).astype(jnp.float32)
        row_target = (owner_of * RBLK + targets).astype(jnp.int32)
        summed = jax.ops.segment_sum(product * alive[:, None, None], row_target, num_segments=nblocks)
        summed = summed.reshape(VERTS, F).astype(jnp.bfloat16)
        conv = jax.nn.relu(jnp.dot(summed, w_conv, preferred_element_type=jnp.float32) + b_conv).astype(jnp.bfloat16)
        gates = jnp.dot(conv, w_input, preferred_element_type=jnp.float32) + jnp.dot(hidden, w_state, preferred_element_type=jnp.float32) + b_gates
        input_gate = jax.nn.sigmoid(gates[:, :HID])
        forget_gate = jax.nn.sigmoid(gates[:, HID:2 * HID] + forget_bias)
        candidate = jnp.tanh(gates[:, 2 * HID:3 * HID])
        output_gate = jax.nn.sigmoid(gates[:, 3 * HID:])
        new_cell = forget_gate * cell + input_gate * candidate
        new_hidden = (output_gate * jnp.tanh(new_cell)).astype(jnp.bfloat16)
        return (new_hidden, new_cell), new_hidden

    start = (jnp.zeros((VERTS, HID), jnp.bfloat16), jnp.zeros((VERTS, HID), jnp.float32))
    _, sequence = lax.scan(advance, start, (features, adjacency_tiles, src_block, dst_block, block_count))
    return sequence
```

```python
import functools

import jax
import jax.numpy as jnp
from jax import lax
from jax.experimental import pallas as pl
from jax.experimental.pallas import tpu as pltpu
from jax.sharding import PartitionSpec as P

MESH = pl.DeviceIdType.MESH
FORGET_BIAS = 2.0
GROUP = 4


def sigmoid(x):
    return 0.5 * jnp.tanh(0.5 * x) + 0.5


def kernel(
    snaps,
    verts,
    feat_hbm,
    adj_hbm,
    src_ref,
    dst_ref,
    count_ref,
    w_conv_hbm,
    b_conv_hbm,
    w_input_hbm,
    w_state_hbm,
    b_gates_hbm,
    out_ref,
    window,
    agg,
    agg_in,
    pre,
    cell,
    hid,
    adj_ref,
    w_conv,
    b_conv_ref,
    w_input,
    w_state,
    b_gates_ref,
    load_sem,
    halo_send,
    halo_recv,
    agg_send,
    agg_recv,
    hid_send,
    hid_recv,
):
    me = lax.axis_index("snap")
    own = lax.axis_index("vert")
    left, right = lax.rem(own + verts - 1, verts), lax.rem(own + 1, verts)
    slots, block, _ = adj_ref.shape
    row_blocks = window.shape[0] // 3
    rows = agg_in.shape[1]
    width = w_state.shape[0]

    loads = [
        pltpu.make_async_copy(feat_hbm, window.at[pl.ds(row_blocks, row_blocks)], load_sem.at[0]),
        pltpu.make_async_copy(adj_hbm, adj_ref, load_sem.at[1]),
        pltpu.make_async_copy(w_conv_hbm, w_conv, load_sem.at[2]),
        pltpu.make_async_copy(b_conv_hbm, b_conv_ref, load_sem.at[3]),
        pltpu.make_async_copy(w_input_hbm, w_input, load_sem.at[4]),
        pltpu.make_async_copy(b_gates_hbm, b_gates_ref, load_sem.at[5]),
        pltpu.make_async_copy(w_state_hbm, w_state, load_sem.at[6]),
    ]
    for load in loads:
        load.start()

    barrier = pltpu.get_barrier_semaphore()
    for near in (left, right):
        pl.semaphore_signal(barrier, inc=1, device_id={"vert": near}, device_id_type=MESH)

    def greet(k, carry):
        peer = lax.rem(me + k, snaps)
        pl.semaphore_signal(barrier, inc=1, device_id={"snap": peer}, device_id_type=MESH)
        return carry

    lax.fori_loop(1, snaps, greet, 0)
    pl.semaphore_wait(barrier, snaps + 1)
    loads[0].wait()

    middle = window.at[pl.ds(row_blocks, row_blocks)]
    halos = [
        pltpu.make_async_remote_copy(
            src_ref=middle,
            dst_ref=window.at[pl.ds(place * row_blocks, row_blocks)],
            send_sem=halo_send.at[i],
            recv_sem=halo_recv.at[i],
            device_id={"vert": near},
            device_id_type=MESH,
        )
        for i, (near, place) in enumerate(((right, 0), (left, 2)))
    ]
    for halo in halos:
        halo.start()
    for halo in halos:
        halo.wait()

    loads[1].wait()

    count = count_ref[0, 0]
    sums = [jnp.zeros((block, block), jnp.float32) for _ in range(row_blocks)]
    for slot in range(slots):
        place = jnp.clip(src_ref[0, slot] - (own - 1) * row_blocks, 0, 3 * row_blocks - 1)
        product = jnp.dot(adj_ref[slot], window[place], preferred_element_type=jnp.float32)
        target = dst_ref[0, slot]
        for r in range(row_blocks):
            taken = jnp.logical_and(target == r, slot < count)
            sums[r] = sums[r] + jnp.where(taken, product, 0.0)
    for r in range(row_blocks):
        agg[pl.ds(r * block, block), :] = sums[r].astype(agg.dtype)

    def agg_copy(k):
        peer = lax.rem(me + k, snaps)
        return pltpu.make_async_remote_copy(
            src_ref=agg.at[pl.ds(pl.multiple_of(peer * rows, rows), rows)],
            dst_ref=agg_in.at[me],
            send_sem=agg_send.at[k],
            recv_sem=agg_recv.at[me],
            device_id={"snap": peer},
            device_id_type=MESH,
        )

    def send_agg(k, carry):
        agg_copy(k).start()
        return carry

    lax.fori_loop(1, snaps, send_agg, 0)
    agg_in[me] = agg[pl.ds(pl.multiple_of(me * rows, rows), rows), :]

    def arrived(buffer, sem, index):
        return pltpu.make_async_remote_copy(
            src_ref=buffer,
            dst_ref=buffer,
            send_sem=sem.at[index],
            recv_sem=sem.at[index],
            device_id={"snap": lax.rem(me + 1, snaps)},
            device_id_type=MESH,
        )

    def hid_copy(step):
        return pltpu.make_async_remote_copy(
            src_ref=hid.at[step],
            dst_ref=out_ref.at[pl.ds(pl.multiple_of(me * rows, rows), rows)],
            send_sem=hid_send.at[step],
            recv_sem=hid_recv.at[me],
            device_id={"snap": step},
            device_id_type=MESH,
        )

    cell[...] = jnp.zeros_like(cell)
    for load in loads[2:]:
        load.wait()

    for first in range(0, snaps, GROUP):
        for t in range(first, first + GROUP):

            @pl.when(me != t)
            def _():
                arrived(agg_in.at[t], agg_recv, t).wait_recv()

        taken = agg_in[pl.ds(first, GROUP)].reshape(GROUP * rows, block)
        conv = jnp.dot(taken, w_conv[...], preferred_element_type=jnp.float32)
        conv = jnp.maximum(conv + b_conv_ref[...], 0.0).astype(jnp.bfloat16)
        for gate in range(4):
            columns = pl.ds(gate * width, width)
            part = jnp.dot(conv, w_input[:, columns], preferred_element_type=jnp.float32)
            part = part + b_gates_ref[:, columns]
            pre[:, :, columns] = part.reshape(GROUP, rows, width)

        def step_body(t, carry):
            local = t - first
            last = hid[lax.rem(t + snaps - 1, snaps)]
            if first == 0:
                last = jnp.where(t == 0, jnp.zeros_like(last), last)
            half = width // 2
            for c in range(2):
                gates = []
                for gate in range(4):
                    columns = pl.ds(gate * width + c * half, half)
                    gates.append(
                        pre[local, :, columns]
                        + jnp.dot(last, w_state[:, columns], preferred_element_type=jnp.float32)
                    )
                columns = pl.ds(c * half, half)
                new_cell = sigmoid(gates[1] + FORGET_BIAS) * cell[:, columns]
                new_cell = new_cell + sigmoid(gates[0]) * jnp.tanh(gates[2])
                cell[:, columns] = new_cell
                new_hidden = sigmoid(gates[3]) * jnp.tanh(new_cell)
                hid[t, :, columns] = new_hidden.astype(hid.dtype)

            @pl.when(me != t)
            def _():
                hid_copy(t).start()

            return carry

        lax.fori_loop(first, first + GROUP, step_body, 0)

    out_ref[pl.ds(pl.multiple_of(me * rows, rows), rows), :] = hid[me]

    def finish(k, carry):
        peer = lax.rem(me + k, snaps)
        agg_copy(k).wait_send()
        arrived(out_ref.at[pl.ds(pl.multiple_of(peer * rows, rows), rows)], hid_recv, peer).wait_recv()
        hid_copy(peer).wait_send()
        return carry

    lax.fori_loop(1, snaps, finish, 0)


def shards(
    snaps,
    verts,
    features,
    adjacency_tiles,
    src_block,
    dst_block,
    block_count,
    w_conv,
    b_conv,
    w_input,
    w_state,
    b_gates,
):
    _, vert_rows, feat = features.shape
    _, slots, block, _ = adjacency_tiles.shape
    out_width = w_conv.shape[1]
    width = w_state.shape[0]
    row_blocks = vert_rows // block
    rows = vert_rows // snaps
    vmem = pl.BlockSpec(memory_space=pltpu.VMEM)
    smem = pl.BlockSpec(memory_space=pltpu.SMEM)
    hbm = pl.BlockSpec(memory_space=pltpu.HBM)
    bf16, f32 = jnp.bfloat16, jnp.float32
    out = pl.pallas_call(
        functools.partial(kernel, snaps, verts),
        out_shape=jax.ShapeDtypeStruct((vert_rows, width), bf16),
        in_specs=[hbm, hbm, smem, smem, smem, hbm, hbm, hbm, hbm, hbm],
        out_specs=vmem,
        scratch_shapes=[
            pltpu.VMEM((3 * row_blocks, block, feat), bf16),
            pltpu.VMEM((vert_rows, feat), bf16),
            pltpu.VMEM((snaps, rows, feat), bf16),
            pltpu.VMEM((GROUP, rows, 4 * width), f32),
            pltpu.VMEM((rows, width), f32),
            pltpu.VMEM((snaps, rows, width), bf16),
            pltpu.VMEM((slots, block, block), bf16),
            pltpu.VMEM((feat, out_width), bf16),
            pltpu.VMEM((1, out_width), f32),
            pltpu.VMEM((out_width, 4 * width), bf16),
            pltpu.VMEM((width, 4 * width), bf16),
            pltpu.VMEM((1, 4 * width), f32),
            pltpu.SemaphoreType.DMA((7,)),
            pltpu.SemaphoreType.DMA((2,)),
            pltpu.SemaphoreType.DMA((2,)),
            pltpu.SemaphoreType.DMA((snaps,)),
            pltpu.SemaphoreType.DMA((snaps,)),
            pltpu.SemaphoreType.DMA((snaps,)),
            pltpu.SemaphoreType.DMA((snaps,)),
        ],
        compiler_params=pltpu.CompilerParams(
            collective_id=0, has_side_effects=True, vmem_limit_bytes=60 * 1024 * 1024
        ),
        cost_estimate=pl.CostEstimate(
            flops=4 * vert_rows * width * 4 * width, bytes_accessed=6_000_000, transcendentals=0
        ),
    )(
        features.reshape(row_blocks, block, feat),
        adjacency_tiles[0],
        src_block,
        dst_block,
        block_count,
        w_conv,
        b_conv[None],
        w_input,
        w_state,
        b_gates[None],
    )
    return out[None]


def solution(mesh):
    placed = (
        P("snap", "vert", None),
        P("snap", "vert", None, None),
        P("snap", "vert"),
        P("snap", "vert"),
        P("snap", "vert"),
        P(),
        P(),
        P(),
        P(),
        P(),
    )
    return jax.shard_map(
        functools.partial(shards, mesh.shape["snap"], mesh.shape["vert"]),
        mesh=mesh,
        in_specs=placed,
        out_specs=P("snap", "vert", None),
        check_vma=False,
    )
```

```python
import functools

import jax
import jax.numpy as jnp
from jax import lax
from jax.experimental import pallas as pl
from jax.experimental.pallas import tpu as pltpu
from jax.sharding import PartitionSpec as P

MESH = pl.DeviceIdType.MESH
FORGET_BIAS = 2.0
GROUP = 4


def sigmoid(x):
    return 0.5 * jnp.tanh(0.5 * x) + 0.5


def kernel(
    snaps,
    verts,
    feat_hbm,
    adj_hbm,
    src_ref,
    dst_ref,
    count_ref,
    w_conv_hbm,
    b_conv_hbm,
    w_input_hbm,
    w_state_hbm,
    b_gates_hbm,
    out_ref,
    window,
    agg,
    agg_in,
    pre,
    cell,
    hid,
    adj_ref,
    w_conv,
    b_conv_ref,
    w_input,
    w_state,
    b_gates_ref,
    known,
    load_sem,
    halo_send,
    halo_recv,
    agg_send,
    agg_recv,
    hid_send,
    hid_recv,
):
    me = lax.axis_index("snap")
    own = lax.axis_index("vert")
    left, right = lax.rem(own + verts - 1, verts), lax.rem(own + 1, verts)
    slots, block, _ = adj_ref.shape
    row_blocks = window.shape[0] // 3
    rows = agg_in.shape[1]
    width = w_state.shape[0]

    loads = [
        pltpu.make_async_copy(feat_hbm, window.at[pl.ds(row_blocks, row_blocks)], load_sem.at[0]),
        pltpu.make_async_copy(adj_hbm, adj_ref, load_sem.at[1]),
        pltpu.make_async_copy(w_conv_hbm, w_conv, load_sem.at[2]),
        pltpu.make_async_copy(b_conv_hbm, b_conv_ref, load_sem.at[3]),
        pltpu.make_async_copy(w_input_hbm, w_input, load_sem.at[4]),
        pltpu.make_async_copy(b_gates_hbm, b_gates_ref, load_sem.at[5]),
        pltpu.make_async_copy(w_state_hbm, w_state, load_sem.at[6]),
    ]
    for load in loads:
        load.start()

    barrier = pltpu.get_barrier_semaphore()
    for near in (left, right):
        pl.semaphore_signal(barrier, inc=1, device_id={"vert": near}, device_id_type=MESH)
    for near in (1, snaps - 1):
        pl.semaphore_signal(
            barrier, inc=1, device_id={"snap": lax.rem(me + near, snaps)}, device_id_type=MESH
        )
    pl.semaphore_wait(barrier, 4)
    loads[0].wait()

    middle = window.at[pl.ds(row_blocks, row_blocks)]
    halos = [
        pltpu.make_async_remote_copy(
            src_ref=middle,
            dst_ref=window.at[pl.ds(place * row_blocks, row_blocks)],
            send_sem=halo_send.at[i],
            recv_sem=halo_recv.at[i],
            device_id={"vert": near},
            device_id_type=MESH,
        )
        for i, (near, place) in enumerate(((right, 0), (left, 2)))
    ]
    for halo in halos:
        halo.start()

    for turn, step in enumerate((1, 2, 4)):
        for side, near in enumerate((step, snaps - step)):
            pl.semaphore_signal(
                known.at[turn, side],
                inc=1,
                device_id={"snap": lax.rem(me + near, snaps)},
                device_id_type=MESH,
            )
        for side in range(2):
            pl.semaphore_wait(known.at[turn, side], 1)

    for halo in halos:
        halo.wait()

    loads[1].wait()

    count = count_ref[0, 0]
    sums = [jnp.zeros((block, block), jnp.float32) for _ in range(row_blocks)]
    for slot in range(slots):
        place = jnp.clip(src_ref[0, slot] - (own - 1) * row_blocks, 0, 3 * row_blocks - 1)
        product = jnp.dot(adj_ref[slot], window[place], preferred_element_type=jnp.float32)
        target = dst_ref[0, slot]
        for r in range(row_blocks):
            taken = jnp.logical_and(target == r, slot < count)
            sums[r] = sums[r] + jnp.where(taken, product, 0.0)
    for r in range(row_blocks):
        agg[pl.ds(r * block, block), :] = sums[r].astype(agg.dtype)

    def agg_copy(k):
        peer = lax.rem(me + k, snaps)
        return pltpu.make_async_remote_copy(
            src_ref=agg.at[pl.ds(pl.multiple_of(peer * rows, rows), rows)],
            dst_ref=agg_in.at[me],
            send_sem=agg_send.at[k],
            recv_sem=agg_recv.at[me],
            device_id={"snap": peer},
            device_id_type=MESH,
        )

    def send_agg(k, carry):
        agg_copy(k).start()
        return carry

    lax.fori_loop(1, snaps, send_agg, 0)
    agg_in[me] = agg[pl.ds(pl.multiple_of(me * rows, rows), rows), :]

    def arrived(buffer, sem, index):
        return pltpu.make_async_remote_copy(
            src_ref=buffer,
            dst_ref=buffer,
            send_sem=sem.at[index],
            recv_sem=sem.at[index],
            device_id={"snap": lax.rem(me + 1, snaps)},
            device_id_type=MESH,
        )

    def hid_copy(step):
        return pltpu.make_async_remote_copy(
            src_ref=hid.at[step],
            dst_ref=out_ref.at[pl.ds(pl.multiple_of(me * rows, rows), rows)],
            send_sem=hid_send.at[step],
            recv_sem=hid_recv.at[me],
            device_id={"snap": step},
            device_id_type=MESH,
        )

    cell[...] = jnp.zeros_like(cell)
    for load in loads[2:]:
        load.wait()

    for first in range(0, snaps, GROUP):
        for t in range(first, first + GROUP):

            @pl.when(me != t)
            def _():
                arrived(agg_in.at[t], agg_recv, t).wait_recv()

        taken = agg_in[pl.ds(first, GROUP)].reshape(GROUP * rows, block)
        conv = jnp.dot(taken, w_conv[...], preferred_element_type=jnp.float32)
        conv = jnp.maximum(conv + b_conv_ref[...], 0.0).astype(jnp.bfloat16)
        for gate in range(4):
            columns = pl.ds(gate * width, width)
            part = jnp.dot(conv, w_input[:, columns], preferred_element_type=jnp.float32)
            part = part + b_gates_ref[:, columns]
            pre[:, :, columns] = part.reshape(GROUP, rows, width)

        def step_body(t, carry):
            local = t - first
            last = hid[lax.rem(t + snaps - 1, snaps)]
            if first == 0:
                last = jnp.where(t == 0, jnp.zeros_like(last), last)
            half = width // 2
            for c in range(2):
                gates = []
                for gate in range(4):
                    columns = pl.ds(gate * width + c * half, half)
                    gates.append(
                        pre[local, :, columns]
                        + jnp.dot(last, w_state[:, columns], preferred_element_type=jnp.float32)
                    )
                columns = pl.ds(c * half, half)
                new_cell = sigmoid(gates[1] + FORGET_BIAS) * cell[:, columns]
                new_cell = new_cell + sigmoid(gates[0]) * jnp.tanh(gates[2])
                cell[:, columns] = new_cell
                new_hidden = sigmoid(gates[3]) * jnp.tanh(new_cell)
                hid[t, :, columns] = new_hidden.astype(hid.dtype)

            @pl.when(me != t)
            def _():
                hid_copy(t).start()

            return carry

        lax.fori_loop(first, first + GROUP, step_body, 0)

    out_ref[pl.ds(pl.multiple_of(me * rows, rows), rows), :] = hid[me]

    def finish(k, carry):
        peer = lax.rem(me + k, snaps)
        agg_copy(k).wait_send()
        arrived(out_ref.at[pl.ds(pl.multiple_of(peer * rows, rows), rows)], hid_recv, peer).wait_recv()
        hid_copy(peer).wait_send()
        return carry

    lax.fori_loop(1, snaps, finish, 0)


def shards(
    snaps,
    verts,
    features,
    adjacency_tiles,
    src_block,
    dst_block,
    block_count,
    w_conv,
    b_conv,
    w_input,
    w_state,
    b_gates,
):
    _, vert_rows, feat = features.shape
    _, slots, block, _ = adjacency_tiles.shape
    out_width = w_conv.shape[1]
    width = w_state.shape[0]
    row_blocks = vert_rows // block
    rows = vert_rows // snaps
    vmem = pl.BlockSpec(memory_space=pltpu.VMEM)
    smem = pl.BlockSpec(memory_space=pltpu.SMEM)
    hbm = pl.BlockSpec(memory_space=pltpu.HBM)
    bf16, f32 = jnp.bfloat16, jnp.float32
    out = pl.pallas_call(
        functools.partial(kernel, snaps, verts),
        out_shape=jax.ShapeDtypeStruct((vert_rows, width), bf16),
        in_specs=[hbm, hbm, smem, smem, smem, hbm, hbm, hbm, hbm, hbm],
        out_specs=vmem,
        scratch_shapes=[
            pltpu.VMEM((3 * row_blocks, block, feat), bf16),
            pltpu.VMEM((vert_rows, feat), bf16),
            pltpu.VMEM((snaps, rows, feat), bf16),
            pltpu.VMEM((GROUP, rows, 4 * width), f32),
            pltpu.VMEM((rows, width), f32),
            pltpu.VMEM((snaps, rows, width), bf16),
            pltpu.VMEM((slots, block, block), bf16),
            pltpu.VMEM((feat, out_width), bf16),
            pltpu.VMEM((1, out_width), f32),
            pltpu.VMEM((out_width, 4 * width), bf16),
            pltpu.VMEM((width, 4 * width), bf16),
            pltpu.VMEM((1, 4 * width), f32),
            pltpu.SemaphoreType.REGULAR((3, 2)),
            pltpu.SemaphoreType.DMA((7,)),
            pltpu.SemaphoreType.DMA((2,)),
            pltpu.SemaphoreType.DMA((2,)),
            pltpu.SemaphoreType.DMA((snaps,)),
            pltpu.SemaphoreType.DMA((snaps,)),
            pltpu.SemaphoreType.DMA((snaps,)),
            pltpu.SemaphoreType.DMA((snaps,)),
        ],
        compiler_params=pltpu.CompilerParams(
            collective_id=0, has_side_effects=True, vmem_limit_bytes=60 * 1024 * 1024
        ),
        cost_estimate=pl.CostEstimate(
            flops=4 * vert_rows * width * 4 * width, bytes_accessed=6_000_000, transcendentals=0
        ),
    )(
        features.reshape(row_blocks, block, feat),
        adjacency_tiles[0],
        src_block,
        dst_block,
        block_count,
        w_conv,
        b_conv[None],
        w_input,
        w_state,
        b_gates[None],
    )
    return out[None]


def solution(mesh):
    placed = (
        P("snap", "vert", None),
        P("snap", "vert", None, None),
        P("snap", "vert"),
        P("snap", "vert"),
        P("snap", "vert"),
        P(),
        P(),
        P(),
        P(),
        P(),
    )
    return jax.shard_map(
        functools.partial(shards, mesh.shape["snap"], mesh.shape["vert"]),
        mesh=mesh,
        in_specs=placed,
        out_specs=P("snap", "vert", None),
        check_vma=False,
    )
```

```python
import functools

import jax
import jax.numpy as jnp
from jax import lax
from jax.experimental import pallas as pl
from jax.experimental.pallas import tpu as pltpu
from jax.sharding import PartitionSpec as P

MESH = pl.DeviceIdType.MESH
FORGET_BIAS = 2.0
GROUP = 4
PARTS = ((0, 16), (16, 32))


def sigmoid(x):
    return 0.5 * jnp.tanh(0.5 * x) + 0.5


def kernel(
    snaps,
    verts,
    feat_hbm,
    adj_hbm,
    src_ref,
    dst_ref,
    count_ref,
    w_conv_hbm,
    b_conv_hbm,
    w_input_hbm,
    w_state_hbm,
    b_gates_hbm,
    out_ref,
    window,
    agg,
    agg_in,
    pre,
    cell,
    hid,
    adj_ref,
    w_conv,
    b_conv_ref,
    w_input,
    w_state,
    b_gates_ref,
    known,
    load_sem,
    halo_send,
    halo_recv,
    agg_send,
    agg_recv,
    hid_send,
    hid_recv,
):
    me = lax.axis_index("snap")
    own = lax.axis_index("vert")
    left, right = lax.rem(own + verts - 1, verts), lax.rem(own + 1, verts)
    slots, block, _ = adj_ref.shape
    row_blocks = window.shape[0] // 3
    rows = agg_in.shape[1]
    width = w_state.shape[0]

    loads = [
        pltpu.make_async_copy(feat_hbm, window.at[pl.ds(row_blocks, row_blocks)], load_sem.at[0]),
        pltpu.make_async_copy(adj_hbm, adj_ref, load_sem.at[1]),
        pltpu.make_async_copy(w_conv_hbm, w_conv, load_sem.at[2]),
        pltpu.make_async_copy(b_conv_hbm, b_conv_ref, load_sem.at[3]),
        pltpu.make_async_copy(w_input_hbm, w_input, load_sem.at[4]),
        pltpu.make_async_copy(b_gates_hbm, b_gates_ref, load_sem.at[5]),
        pltpu.make_async_copy(w_state_hbm, w_state, load_sem.at[6]),
    ]
    for load in loads:
        load.start()

    def over_snap(step):
        return {"snap": lax.rem(me + step, snaps)}

    barrier = pltpu.get_barrier_semaphore()
    for near in (left, right):
        pl.semaphore_signal(barrier, inc=1, device_id={"vert": near}, device_id_type=MESH)
    for near in (2, snaps - 2, 1, snaps - 1):
        pl.semaphore_signal(barrier, inc=1, device_id=over_snap(near), device_id_type=MESH)
    pl.semaphore_wait(barrier, 6)
    loads[0].wait()

    middle = window.at[pl.ds(row_blocks, row_blocks)]
    halos = [
        pltpu.make_async_remote_copy(
            src_ref=middle,
            dst_ref=window.at[pl.ds(place * row_blocks, row_blocks)],
            send_sem=halo_send.at[i],
            recv_sem=halo_recv.at[i],
            device_id={"vert": near},
            device_id_type=MESH,
        )
        for i, (near, place) in enumerate(((right, 0), (left, 2)))
    ]
    for halo in halos:
        halo.start()

    def tell(turn, step):
        for side, near in enumerate((step, snaps - step)):
            pl.semaphore_signal(
                known.at[turn, side], inc=1, device_id=over_snap(near), device_id_type=MESH
            )

    def hear(turn):
        for side in range(2):
            pl.semaphore_wait(known.at[turn, side], 1)

    tell(0, 2)
    hear(0)
    tell(1, 4)

    for halo in halos:
        halo.wait()

    loads[1].wait()

    count = count_ref[0, 0]
    sums = [jnp.zeros((block, block), jnp.float32) for _ in range(row_blocks)]
    for slot in range(slots):
        place = jnp.clip(src_ref[0, slot] - (own - 1) * row_blocks, 0, 3 * row_blocks - 1)
        product = jnp.dot(adj_ref[slot], window[place], preferred_element_type=jnp.float32)
        target = dst_ref[0, slot]
        for r in range(row_blocks):
            taken = jnp.logical_and(target == r, slot < count)
            sums[r] = sums[r] + jnp.where(taken, product, 0.0)
    for r in range(row_blocks):
        agg[pl.ds(r * block, block), :] = sums[r].astype(agg.dtype)

    def agg_copy(part, k):
        start, size = PARTS[part]
        peer = lax.rem(me + k, snaps)
        return pltpu.make_async_remote_copy(
            src_ref=agg.at[pl.ds(pl.multiple_of(peer * rows + start, 16), size)],
            dst_ref=agg_in.at[me, pl.ds(start, size)],
            send_sem=agg_send.at[part, k],
            recv_sem=agg_recv.at[part, me],
            device_id={"snap": peer},
            device_id_type=MESH,
        )

    def send_agg(part, first, last):
        def both_ways(k, carry):
            agg_copy(part, k).start()
            agg_copy(part, snaps - k).start()
            return carry

        lax.fori_loop(first, last, both_ways, 0)

    half_way = snaps // 2
    send_agg(0, 1, 5)
    hear(1)
    send_agg(0, 5, half_way)
    agg_copy(0, half_way).start()
    send_agg(1, 1, half_way)
    agg_copy(1, half_way).start()
    agg_in[me] = agg[pl.ds(pl.multiple_of(me * rows, rows), rows), :]

    def arrived(buffer, sem):
        return pltpu.make_async_remote_copy(
            src_ref=buffer,
            dst_ref=buffer,
            send_sem=sem,
            recv_sem=sem,
            device_id=over_snap(1),
            device_id_type=MESH,
        )

    def hid_copy(part, step):
        start, size = PARTS[part]
        return pltpu.make_async_remote_copy(
            src_ref=hid.at[step, pl.ds(start, size)],
            dst_ref=out_ref.at[pl.ds(pl.multiple_of(me * rows + start, 16), size)],
            send_sem=hid_send.at[part, step],
            recv_sem=hid_recv.at[part, me],
            device_id={"snap": step},
            device_id_type=MESH,
        )

    cell[...] = jnp.zeros_like(cell)
    for load in loads[2:]:
        load.wait()

    def step_body(part, first, t, carry):
        start, size = PARTS[part]
        lines = pl.ds(start, size)
        local = t - first
        last = hid[lax.rem(t + snaps - 1, snaps), lines, :]
        if first == 0:
            last = jnp.where(t == 0, jnp.zeros_like(last), last)
        half = width // 2
        for c in range(2):
            gates = []
            for gate in range(4):
                columns = pl.ds(gate * width + c * half, half)
                gates.append(
                    pre[pl.ds(pl.multiple_of(local * size, size), size), columns]
                    + jnp.dot(last, w_state[:, columns], preferred_element_type=jnp.float32)
                )
            columns = pl.ds(c * half, half)
            new_cell = sigmoid(gates[1] + FORGET_BIAS) * cell[lines, columns]
            new_cell = new_cell + sigmoid(gates[0]) * jnp.tanh(gates[2])
            cell[lines, columns] = new_cell
            new_hidden = sigmoid(gates[3]) * jnp.tanh(new_cell)
            hid[t, lines, columns] = new_hidden.astype(hid.dtype)

        @pl.when(me != t)
        def _():
            hid_copy(part, t).start()

        return carry

    for part, (start, size) in enumerate(PARTS):
        lines = pl.ds(start, size)
        for first in range(0, snaps, GROUP):
            for t in range(first, first + GROUP):

                @pl.when(me != t)
                def _():
                    arrived(agg_in.at[t, lines], agg_recv.at[part, t]).wait_recv()

            taken = agg_in[pl.ds(first, GROUP), lines, :].reshape(GROUP * size, block)
            conv = jnp.dot(taken, w_conv[...], preferred_element_type=jnp.float32)
            conv = jnp.maximum(conv + b_conv_ref[...], 0.0).astype(jnp.bfloat16)
            for gate in range(4):
                columns = pl.ds(gate * width, width)
                product = jnp.dot(conv, w_input[:, columns], preferred_element_type=jnp.float32)
                pre[pl.ds(0, GROUP * size), columns] = product + b_gates_ref[:, columns]
            lax.fori_loop(first, first + GROUP, functools.partial(step_body, part, first), 0)

    out_ref[pl.ds(pl.multiple_of(me * rows, rows), rows), :] = hid[me]

    def finish(part, k, carry):
        start, size = PARTS[part]
        peer = lax.rem(me + k, snaps)
        agg_copy(part, k).wait_send()
        lines = pl.ds(pl.multiple_of(peer * rows + start, 16), size)
        arrived(out_ref.at[lines], hid_recv.at[part, peer]).wait_recv()
        hid_copy(part, peer).wait_send()
        return carry

    for part in range(len(PARTS)):
        lax.fori_loop(1, snaps, functools.partial(finish, part), 0)


def shards(
    snaps,
    verts,
    features,
    adjacency_tiles,
    src_block,
    dst_block,
    block_count,
    w_conv,
    b_conv,
    w_input,
    w_state,
    b_gates,
):
    _, vert_rows, feat = features.shape
    _, slots, block, _ = adjacency_tiles.shape
    out_width = w_conv.shape[1]
    width = w_state.shape[0]
    row_blocks = vert_rows // block
    rows = vert_rows // snaps
    vmem = pl.BlockSpec(memory_space=pltpu.VMEM)
    smem = pl.BlockSpec(memory_space=pltpu.SMEM)
    hbm = pl.BlockSpec(memory_space=pltpu.HBM)
    bf16, f32 = jnp.bfloat16, jnp.float32
    out = pl.pallas_call(
        functools.partial(kernel, snaps, verts),
        out_shape=jax.ShapeDtypeStruct((vert_rows, width), bf16),
        in_specs=[hbm, hbm, smem, smem, smem, hbm, hbm, hbm, hbm, hbm],
        out_specs=vmem,
        scratch_shapes=[
            pltpu.VMEM((3 * row_blocks, block, feat), bf16),
            pltpu.VMEM((vert_rows, feat), bf16),
            pltpu.VMEM((snaps, rows, feat), bf16),
            pltpu.VMEM((GROUP * rows, 4 * width), f32),
            pltpu.VMEM((rows, width), f32),
            pltpu.VMEM((snaps, rows, width), bf16),
            pltpu.VMEM((slots, block, block), bf16),
            pltpu.VMEM((feat, out_width), bf16),
            pltpu.VMEM((1, out_width), f32),
            pltpu.VMEM((out_width, 4 * width), bf16),
            pltpu.VMEM((width, 4 * width), bf16),
            pltpu.VMEM((1, 4 * width), f32),
            pltpu.SemaphoreType.REGULAR((2, 2)),
            pltpu.SemaphoreType.DMA((7,)),
            pltpu.SemaphoreType.DMA((2,)),
            pltpu.SemaphoreType.DMA((2,)),
            pltpu.SemaphoreType.DMA((len(PARTS), snaps)),
            pltpu.SemaphoreType.DMA((len(PARTS), snaps)),
            pltpu.SemaphoreType.DMA((len(PARTS), snaps)),
            pltpu.SemaphoreType.DMA((len(PARTS), snaps)),
        ],
        compiler_params=pltpu.CompilerParams(
            collective_id=0, has_side_effects=True, vmem_limit_bytes=60 * 1024 * 1024
        ),
        cost_estimate=pl.CostEstimate(
            flops=4 * vert_rows * width * 4 * width, bytes_accessed=6_000_000, transcendentals=0
        ),
    )(
        features.reshape(row_blocks, block, feat),
        adjacency_tiles[0],
        src_block,
        dst_block,
        block_count,
        w_conv,
        b_conv[None],
        w_input,
        w_state,
        b_gates[None],
    )
    return out[None]


def solution(mesh):
    placed = (
        P("snap", "vert", None),
        P("snap", "vert", None, None),
        P("snap", "vert"),
        P("snap", "vert"),
        P("snap", "vert"),
        P(),
        P(),
        P(),
        P(),
        P(),
    )
    return jax.shard_map(
        functools.partial(shards, mesh.shape["snap"], mesh.shape["vert"]),
        mesh=mesh,
        in_specs=placed,
        out_specs=P("snap", "vert", None),
        check_vma=False,
    )
```

```python
import functools

import jax
import jax.numpy as jnp
from jax import lax
from jax.experimental import pallas as pl
from jax.experimental.pallas import tpu as pltpu
from jax.sharding import PartitionSpec as P

MESH = pl.DeviceIdType.MESH
FORGET_BIAS = 2.0
GROUP = 4
PARTS = ((0, 16), (16, 32))


def sigmoid(x):
    return 0.5 * jnp.tanh(0.5 * x) + 0.5


def kernel(
    snaps,
    verts,
    feat_hbm,
    adj_hbm,
    src_ref,
    dst_ref,
    count_ref,
    w_conv_hbm,
    b_conv_hbm,
    w_input_hbm,
    w_state_hbm,
    b_gates_hbm,
    out_ref,
    window,
    agg,
    agg_in,
    pre,
    cell,
    hid,
    adj_ref,
    w_conv,
    b_conv_ref,
    w_input,
    w_state,
    b_gates_ref,
    known,
    load_sem,
    halo_send,
    halo_recv,
    agg_send,
    agg_recv,
    hid_send,
    hid_recv,
):
    me = lax.axis_index("snap")
    own = lax.axis_index("vert")
    left, right = lax.rem(own + verts - 1, verts), lax.rem(own + 1, verts)
    slots, block, _ = adj_ref.shape
    row_blocks = window.shape[0] // 3
    rows = agg_in.shape[1]
    width = w_state.shape[0]

    loads = [
        pltpu.make_async_copy(feat_hbm, window.at[pl.ds(row_blocks, row_blocks)], load_sem.at[0]),
        pltpu.make_async_copy(adj_hbm, adj_ref, load_sem.at[1]),
        pltpu.make_async_copy(w_conv_hbm, w_conv, load_sem.at[2]),
        pltpu.make_async_copy(b_conv_hbm, b_conv_ref, load_sem.at[3]),
        pltpu.make_async_copy(w_input_hbm, w_input, load_sem.at[4]),
        pltpu.make_async_copy(b_gates_hbm, b_gates_ref, load_sem.at[5]),
        pltpu.make_async_copy(w_state_hbm, w_state, load_sem.at[6]),
    ]
    for load in loads:
        load.start()

    def over_snap(step):
        return {"snap": lax.rem(me + step, snaps)}

    barrier = pltpu.get_barrier_semaphore()
    for near in (left, right):
        pl.semaphore_signal(barrier, inc=1, device_id={"vert": near}, device_id_type=MESH)
    for near in (2, snaps - 2, 1, snaps - 1):
        pl.semaphore_signal(barrier, inc=1, device_id=over_snap(near), device_id_type=MESH)
    pl.semaphore_wait(barrier, 6)
    loads[0].wait()

    middle = window.at[pl.ds(row_blocks, row_blocks)]
    halos = [
        pltpu.make_async_remote_copy(
            src_ref=middle,
            dst_ref=window.at[pl.ds(place * row_blocks, row_blocks)],
            send_sem=halo_send.at[i],
            recv_sem=halo_recv.at[i],
            device_id={"vert": near},
            device_id_type=MESH,
        )
        for i, (near, place) in enumerate(((right, 0), (left, 2)))
    ]
    for halo in halos:
        halo.start()

    def tell(turn, step):
        for side, near in enumerate((step, snaps - step)):
            pl.semaphore_signal(
                known.at[turn, side], inc=1, device_id=over_snap(near), device_id_type=MESH
            )

    def hear(turn):
        for side in range(2):
            pl.semaphore_wait(known.at[turn, side], 1)

    tell(0, 2)
    hear(0)
    tell(1, 4)

    for halo in halos:
        halo.wait()

    loads[1].wait()

    count = count_ref[0, 0]
    sums = [jnp.zeros((block, block), jnp.float32) for _ in range(row_blocks)]
    for slot in range(slots):
        place = jnp.clip(src_ref[0, slot] - (own - 1) * row_blocks, 0, 3 * row_blocks - 1)
        product = jnp.dot(adj_ref[slot], window[place], preferred_element_type=jnp.float32)
        target = dst_ref[0, slot]
        for r in range(row_blocks):
            taken = jnp.logical_and(target == r, slot < count)
            sums[r] = sums[r] + jnp.where(taken, product, 0.0)
    for r in range(row_blocks):
        agg[pl.ds(r * block, block), :] = sums[r].astype(agg.dtype)

    def agg_copy(part, k):
        start, size = PARTS[part]
        peer = lax.rem(me + k, snaps)
        return pltpu.make_async_remote_copy(
            src_ref=agg.at[pl.ds(pl.multiple_of(peer * rows + start, 16), size)],
            dst_ref=agg_in.at[me, pl.ds(start, size)],
            send_sem=agg_send.at[part, k],
            recv_sem=agg_recv.at[part, me],
            device_id={"snap": peer},
            device_id_type=MESH,
        )

    def send_agg(part, first, last):
        def both_ways(k, carry):
            agg_copy(part, k).start()
            agg_copy(part, snaps - k).start()
            return carry

        lax.fori_loop(first, last, both_ways, 0)

    half_way = snaps // 2
    send_agg(0, 1, 5)
    hear(1)
    send_agg(0, 5, half_way)
    agg_copy(0, half_way).start()
    send_agg(1, 1, half_way)
    agg_copy(1, half_way).start()
    agg_in[me] = agg[pl.ds(pl.multiple_of(me * rows, rows), rows), :]

    def arrived(buffer, sem):
        return pltpu.make_async_remote_copy(
            src_ref=buffer,
            dst_ref=buffer,
            send_sem=sem,
            recv_sem=sem,
            device_id=over_snap(1),
            device_id_type=MESH,
        )

    def hid_copy(part, step):
        start, size = PARTS[part]
        return pltpu.make_async_remote_copy(
            src_ref=hid.at[step, pl.ds(start, size)],
            dst_ref=out_ref.at[pl.ds(pl.multiple_of(me * rows + start, 16), size)],
            send_sem=hid_send.at[part, step],
            recv_sem=hid_recv.at[part, me],
            device_id={"snap": step},
            device_id_type=MESH,
        )

    cell[...] = jnp.zeros_like(cell)
    for load in loads[2:]:
        load.wait()

    def step_body(part, first, t, carry):
        start, size = PARTS[part]
        lines = pl.ds(start, size)
        local = t - first
        last = hid[lax.rem(t + snaps - 1, snaps), lines, :]
        if first == 0:
            last = jnp.where(t == 0, jnp.zeros_like(last), last)
        half = width // 2
        for c in range(2):
            gates = []
            for gate in range(4):
                columns = pl.ds(gate * width + c * half, half)
                gates.append(
                    pre[pl.ds(pl.multiple_of(local * size, size), size), columns]
                    + jnp.dot(last, w_state[:, columns], preferred_element_type=jnp.float32)
                )
            columns = pl.ds(c * half, half)
            new_cell = sigmoid(gates[1] + FORGET_BIAS) * cell[lines, columns]
            new_cell = new_cell + sigmoid(gates[0]) * jnp.tanh(gates[2])
            cell[lines, columns] = new_cell
            new_hidden = sigmoid(gates[3]) * jnp.tanh(new_cell)
            hid[t, lines, columns] = new_hidden.astype(hid.dtype)

        @pl.when(me != t)
        def _():
            hid_copy(part, t).start()

        return carry

    for part, (start, size) in enumerate(PARTS):
        lines = pl.ds(start, size)
        for first in range(0, snaps, GROUP):
            for t in range(first, first + GROUP):

                @pl.when(me != t)
                def _():
                    arrived(agg_in.at[t, lines], agg_recv.at[part, t]).wait_recv()

            taken = agg_in[pl.ds(first, GROUP), lines, :].reshape(GROUP * size, block)
            conv = jnp.dot(taken, w_conv[...], preferred_element_type=jnp.float32)
            conv = jnp.maximum(conv + b_conv_ref[...], 0.0).astype(jnp.bfloat16)
            for gate in range(4):
                columns = pl.ds(gate * width, width)
                product = jnp.dot(conv, w_input[:, columns], preferred_element_type=jnp.float32)
                pre[pl.ds(0, GROUP * size), columns] = product + b_gates_ref[:, columns]
            lax.fori_loop(first, first + GROUP, functools.partial(step_body, part, first), 0)

    kept = pltpu.make_async_copy(
        hid.at[me], out_ref.at[pl.ds(pl.multiple_of(me * rows, rows), rows)], load_sem.at[0]
    )
    kept.start()
    kept.wait()

    def finish(part, k, carry):
        start, size = PARTS[part]
        peer = lax.rem(me + k, snaps)
        agg_copy(part, k).wait_send()
        lines = pl.ds(pl.multiple_of(peer * rows + start, 16), size)
        arrived(out_ref.at[lines], hid_recv.at[part, peer]).wait_recv()
        hid_copy(part, peer).wait_send()
        return carry

    for part in range(len(PARTS)):
        lax.fori_loop(1, snaps, functools.partial(finish, part), 0)


def shards(
    snaps,
    verts,
    features,
    adjacency_tiles,
    src_block,
    dst_block,
    block_count,
    w_conv,
    b_conv,
    w_input,
    w_state,
    b_gates,
):
    _, vert_rows, feat = features.shape
    _, slots, block, _ = adjacency_tiles.shape
    out_width = w_conv.shape[1]
    width = w_state.shape[0]
    row_blocks = vert_rows // block
    rows = vert_rows // snaps
    vmem = pl.BlockSpec(memory_space=pltpu.VMEM)
    smem = pl.BlockSpec(memory_space=pltpu.SMEM)
    hbm = pl.BlockSpec(memory_space=pltpu.HBM)
    bf16, f32 = jnp.bfloat16, jnp.float32
    out = pl.pallas_call(
        functools.partial(kernel, snaps, verts),
        out_shape=jax.ShapeDtypeStruct((vert_rows, width), bf16),
        in_specs=[hbm, hbm, smem, smem, smem, hbm, hbm, hbm, hbm, hbm],
        out_specs=hbm,
        scratch_shapes=[
            pltpu.VMEM((3 * row_blocks, block, feat), bf16),
            pltpu.VMEM((vert_rows, feat), bf16),
            pltpu.VMEM((snaps, rows, feat), bf16),
            pltpu.VMEM((GROUP * rows, 4 * width), f32),
            pltpu.VMEM((rows, width), f32),
            pltpu.VMEM((snaps, rows, width), bf16),
            pltpu.VMEM((slots, block, block), bf16),
            pltpu.VMEM((feat, out_width), bf16),
            pltpu.VMEM((1, out_width), f32),
            pltpu.VMEM((out_width, 4 * width), bf16),
            pltpu.VMEM((width, 4 * width), bf16),
            pltpu.VMEM((1, 4 * width), f32),
            pltpu.SemaphoreType.REGULAR((2, 2)),
            pltpu.SemaphoreType.DMA((7,)),
            pltpu.SemaphoreType.DMA((2,)),
            pltpu.SemaphoreType.DMA((2,)),
            pltpu.SemaphoreType.DMA((len(PARTS), snaps)),
            pltpu.SemaphoreType.DMA((len(PARTS), snaps)),
            pltpu.SemaphoreType.DMA((len(PARTS), snaps)),
            pltpu.SemaphoreType.DMA((len(PARTS), snaps)),
        ],
        compiler_params=pltpu.CompilerParams(
            collective_id=0, has_side_effects=True, vmem_limit_bytes=60 * 1024 * 1024
        ),
        cost_estimate=pl.CostEstimate(
            flops=4 * vert_rows * width * 4 * width, bytes_accessed=6_000_000, transcendentals=0
        ),
    )(
        features.reshape(row_blocks, block, feat),
        adjacency_tiles[0],
        src_block,
        dst_block,
        block_count,
        w_conv,
        b_conv[None],
        w_input,
        w_state,
        b_gates[None],
    )
    return out[None]


def solution(mesh):
    placed = (
        P("snap", "vert", None),
        P("snap", "vert", None, None),
        P("snap", "vert"),
        P("snap", "vert"),
        P("snap", "vert"),
        P(),
        P(),
        P(),
        P(),
        P(),
    )
    return jax.shard_map(
        functools.partial(shards, mesh.shape["snap"], mesh.shape["vert"]),
        mesh=mesh,
        in_specs=placed,
        out_specs=P("snap", "vert", None),
        check_vma=False,
    )
```

```python
import functools

import jax
import jax.numpy as jnp
from jax import lax
from jax.experimental import pallas as pl
from jax.experimental.pallas import tpu as pltpu
from jax.sharding import PartitionSpec as P

MESH = pl.DeviceIdType.MESH
FORGET_BIAS = 2.0
GROUP = 4
PARTS = ((0, 16), (16, 32))


def sigmoid(x):
    return 0.5 * jnp.tanh(0.5 * x) + 0.5


def kernel(
    snaps,
    verts,
    feat_hbm,
    adj_hbm,
    src_ref,
    dst_ref,
    count_ref,
    w_conv_hbm,
    b_conv_hbm,
    w_input_hbm,
    w_state_hbm,
    b_gates_hbm,
    out_ref,
    window,
    agg,
    agg_in,
    pre,
    cell,
    hid,
    adj_ref,
    w_conv,
    b_conv_ref,
    w_input,
    w_state,
    b_gates_ref,
    known,
    load_sem,
    halo_send,
    halo_recv,
    agg_send,
    agg_recv,
    hid_send,
    hid_recv,
):
    me = lax.axis_index("snap")
    own = lax.axis_index("vert")
    left, right = lax.rem(own + verts - 1, verts), lax.rem(own + 1, verts)
    slots, block, _ = adj_ref.shape
    row_blocks = window.shape[0] // 3
    rows = agg_in.shape[1]
    width = w_state.shape[0]

    loads = [
        pltpu.make_async_copy(feat_hbm, window.at[pl.ds(row_blocks, row_blocks)], load_sem.at[0]),
        pltpu.make_async_copy(adj_hbm, adj_ref, load_sem.at[1]),
        pltpu.make_async_copy(w_conv_hbm, w_conv, load_sem.at[2]),
        pltpu.make_async_copy(b_conv_hbm, b_conv_ref, load_sem.at[3]),
        pltpu.make_async_copy(w_input_hbm, w_input, load_sem.at[4]),
        pltpu.make_async_copy(b_gates_hbm, b_gates_ref, load_sem.at[5]),
        pltpu.make_async_copy(w_state_hbm, w_state, load_sem.at[6]),
    ]
    for load in loads:
        load.start()

    def over_snap(step):
        return {"snap": lax.rem(me + step, snaps)}

    barrier = pltpu.get_barrier_semaphore()
    for near in (left, right):
        pl.semaphore_signal(barrier, inc=1, device_id={"vert": near}, device_id_type=MESH)
    for near in (4, snaps - 4, 3, snaps - 3, 2, snaps - 2, 1, snaps - 1):
        pl.semaphore_signal(barrier, inc=1, device_id=over_snap(near), device_id_type=MESH)
    pl.semaphore_wait(barrier, 10)
    loads[0].wait()

    middle = window.at[pl.ds(row_blocks, row_blocks)]
    halos = [
        pltpu.make_async_remote_copy(
            src_ref=middle,
            dst_ref=window.at[pl.ds(place * row_blocks, row_blocks)],
            send_sem=halo_send.at[i],
            recv_sem=halo_recv.at[i],
            device_id={"vert": near},
            device_id_type=MESH,
        )
        for i, (near, place) in enumerate(((right, 0), (left, 2)))
    ]
    for halo in halos:
        halo.start()

    def tell(turn, step):
        for side, near in enumerate((step, snaps - step)):
            pl.semaphore_signal(
                known.at[turn, side], inc=1, device_id=over_snap(near), device_id_type=MESH
            )

    def hear(turn):
        for side in range(2):
            pl.semaphore_wait(known.at[turn, side], 1)

    tell(0, 4)

    for halo in halos:
        halo.wait()

    loads[1].wait()

    count = count_ref[0, 0]
    sums = [jnp.zeros((block, block), jnp.float32) for _ in range(row_blocks)]
    for slot in range(slots):
        place = jnp.clip(src_ref[0, slot] - (own - 1) * row_blocks, 0, 3 * row_blocks - 1)
        product = jnp.dot(adj_ref[slot], window[place], preferred_element_type=jnp.float32)
        target = dst_ref[0, slot]
        for r in range(row_blocks):
            taken = jnp.logical_and(target == r, slot < count)
            sums[r] = sums[r] + jnp.where(taken, product, 0.0)
    for r in range(row_blocks):
        agg[pl.ds(r * block, block), :] = sums[r].astype(agg.dtype)

    def agg_copy(part, k):
        start, size = PARTS[part]
        peer = lax.rem(me + k, snaps)
        return pltpu.make_async_remote_copy(
            src_ref=agg.at[pl.ds(pl.multiple_of(peer * rows + start, 16), size)],
            dst_ref=agg_in.at[me, pl.ds(start, size)],
            send_sem=agg_send.at[part, k],
            recv_sem=agg_recv.at[part, me],
            device_id={"snap": peer},
            device_id_type=MESH,
        )

    def send_agg(part, first, last):
        def both_ways(k, carry):
            agg_copy(part, k).start()
            agg_copy(part, snaps - k).start()
            return carry

        lax.fori_loop(first, last, both_ways, 0)

    half_way = snaps // 2
    send_agg(0, 1, 5)
    hear(0)
    send_agg(0, 5, half_way)
    agg_copy(0, half_way).start()
    send_agg(1, 1, half_way)
    agg_copy(1, half_way).start()
    agg_in[me] = agg[pl.ds(pl.multiple_of(me * rows, rows), rows), :]

    def arrived(buffer, sem):
        return pltpu.make_async_remote_copy(
            src_ref=buffer,
            dst_ref=buffer,
            send_sem=sem,
            recv_sem=sem,
            device_id=over_snap(1),
            device_id_type=MESH,
        )

    def hid_copy(part, step):
        start, size = PARTS[part]
        return pltpu.make_async_remote_copy(
            src_ref=hid.at[step, pl.ds(start, size)],
            dst_ref=out_ref.at[pl.ds(pl.multiple_of(me * rows + start, 16), size)],
            send_sem=hid_send.at[part, step],
            recv_sem=hid_recv.at[part, me],
            device_id={"snap": step},
            device_id_type=MESH,
        )

    cell[...] = jnp.zeros_like(cell)
    for load in loads[2:]:
        load.wait()

    def step_body(part, first, t, carry):
        start, size = PARTS[part]
        lines = pl.ds(start, size)
        local = t - first
        last = hid[lax.rem(t + snaps - 1, snaps), lines, :]
        if first == 0:
            last = jnp.where(t == 0, jnp.zeros_like(last), last)
        half = width // 2
        for c in range(2):
            gates = []
            for gate in range(4):
                columns = pl.ds(gate * width + c * half, half)
                gates.append(
                    pre[pl.ds(pl.multiple_of(local * size, size), size), columns]
                    + jnp.dot(last, w_state[:, columns], preferred_element_type=jnp.float32)
                )
            columns = pl.ds(c * half, half)
            new_cell = sigmoid(gates[1] + FORGET_BIAS) * cell[lines, columns]
            new_cell = new_cell + sigmoid(gates[0]) * jnp.tanh(gates[2])
            cell[lines, columns] = new_cell
            new_hidden = sigmoid(gates[3]) * jnp.tanh(new_cell)
            hid[t, lines, columns] = new_hidden.astype(hid.dtype)

        @pl.when(me != t)
        def _():
            hid_copy(part, t).start()

        return carry

    for part, (start, size) in enumerate(PARTS):
        lines = pl.ds(start, size)
        for first in range(0, snaps, GROUP):
            for t in range(first, first + GROUP):

                @pl.when(me != t)
                def _():
                    arrived(agg_in.at[t, lines], agg_recv.at[part, t]).wait_recv()

            taken = agg_in[pl.ds(first, GROUP), lines, :].reshape(GROUP * size, block)
            conv = jnp.dot(taken, w_conv[...], preferred_element_type=jnp.float32)
            conv = jnp.maximum(conv + b_conv_ref[...], 0.0).astype(jnp.bfloat16)
            for gate in range(4):
                columns = pl.ds(gate * width, width)
                product = jnp.dot(conv, w_input[:, columns], preferred_element_type=jnp.float32)
                pre[pl.ds(0, GROUP * size), columns] = product + b_gates_ref[:, columns]
            lax.fori_loop(first, first + GROUP, functools.partial(step_body, part, first), 0)

    kept = pltpu.make_async_copy(
        hid.at[me], out_ref.at[pl.ds(pl.multiple_of(me * rows, rows), rows)], load_sem.at[0]
    )
    kept.start()
    kept.wait()

    def finish(part, k, carry):
        start, size = PARTS[part]
        peer = lax.rem(me + k, snaps)
        agg_copy(part, k).wait_send()
        lines = pl.ds(pl.multiple_of(peer * rows + start, 16), size)
        arrived(out_ref.at[lines], hid_recv.at[part, peer]).wait_recv()
        hid_copy(part, peer).wait_send()
        return carry

    for part in range(len(PARTS)):
        lax.fori_loop(1, snaps, functools.partial(finish, part), 0)


def shards(
    snaps,
    verts,
    features,
    adjacency_tiles,
    src_block,
    dst_block,
    block_count,
    w_conv,
    b_conv,
    w_input,
    w_state,
    b_gates,
):
    _, vert_rows, feat = features.shape
    _, slots, block, _ = adjacency_tiles.shape
    out_width = w_conv.shape[1]
    width = w_state.shape[0]
    row_blocks = vert_rows // block
    rows = vert_rows // snaps
    vmem = pl.BlockSpec(memory_space=pltpu.VMEM)
    smem = pl.BlockSpec(memory_space=pltpu.SMEM)
    hbm = pl.BlockSpec(memory_space=pltpu.HBM)
    bf16, f32 = jnp.bfloat16, jnp.float32
    out = pl.pallas_call(
        functools.partial(kernel, snaps, verts),
        out_shape=jax.ShapeDtypeStruct((vert_rows, width), bf16),
        in_specs=[hbm, hbm, smem, smem, smem, hbm, hbm, hbm, hbm, hbm],
        out_specs=hbm,
        scratch_shapes=[
            pltpu.VMEM((3 * row_blocks, block, feat), bf16),
            pltpu.VMEM((vert_rows, feat), bf16),
            pltpu.VMEM((snaps, rows, feat), bf16),
            pltpu.VMEM((GROUP * rows, 4 * width), f32),
            pltpu.VMEM((rows, width), f32),
            pltpu.VMEM((snaps, rows, width), bf16),
            pltpu.VMEM((slots, block, block), bf16),
            pltpu.VMEM((feat, out_width), bf16),
            pltpu.VMEM((1, out_width), f32),
            pltpu.VMEM((out_width, 4 * width), bf16),
            pltpu.VMEM((width, 4 * width), bf16),
            pltpu.VMEM((1, 4 * width), f32),
            pltpu.SemaphoreType.REGULAR((1, 2)),
            pltpu.SemaphoreType.DMA((7,)),
            pltpu.SemaphoreType.DMA((2,)),
            pltpu.SemaphoreType.DMA((2,)),
            pltpu.SemaphoreType.DMA((len(PARTS), snaps)),
            pltpu.SemaphoreType.DMA((len(PARTS), snaps)),
            pltpu.SemaphoreType.DMA((len(PARTS), snaps)),
            pltpu.SemaphoreType.DMA((len(PARTS), snaps)),
        ],
        compiler_params=pltpu.CompilerParams(
            collective_id=0, has_side_effects=True, vmem_limit_bytes=60 * 1024 * 1024
        ),
        cost_estimate=pl.CostEstimate(
            flops=4 * vert_rows * width * 4 * width, bytes_accessed=6_000_000, transcendentals=0
        ),
    )(
        features.reshape(row_blocks, block, feat),
        adjacency_tiles[0],
        src_block,
        dst_block,
        block_count,
        w_conv,
        b_conv[None],
        w_input,
        w_state,
        b_gates[None],
    )
    return out[None]


def solution(mesh):
    placed = (
        P("snap", "vert", None),
        P("snap", "vert", None, None),
        P("snap", "vert"),
        P("snap", "vert"),
        P("snap", "vert"),
        P(),
        P(),
        P(),
        P(),
        P(),
    )
    return jax.shard_map(
        functools.partial(shards, mesh.shape["snap"], mesh.shape["vert"]),
        mesh=mesh,
        in_specs=placed,
        out_specs=P("snap", "vert", None),
        check_vma=False,
    )
```
